512 devices in a mesh: segment: 16 (over z_hi, y), ctx: 8 (over x, core), mp: 4 (over z_lo).
Axes of the slice: x: 4, y: 8, z: 8 (z_hi: 2, z_lo: 4; z = z_hi * 4 + z_lo), core: 2. Of those that a mesh axis runs over, the one named last changes fastest.
Arguments:
- queries: bfloat16 [16, 2, 1024, 2048], P('segment', None, 'ctx', 'mp')
- enc_states: bfloat16 [2, 2048, 4096], P(None, 'ctx', 'segment'), may hold values from -6 to 6
- key_weight: bfloat16 [16, 4096, 2048], P('segment', 'ctx', 'mp'), may hold values from -0.09375 to 0.09375
- value_weight: bfloat16 [16, 4096, 2048], P('segment', 'ctx', 'mp'), may hold values from -0.09375 to 0.09375
- enc_lengths: int32 [2], replicated, may hold values from 1025 to 2048, as said below
Outputs:
- context: bfloat16 [16, 2, 1024, 2048], P('segment', None, 'ctx', 'mp')
The draws below stay inside these ranges and needn't reach their ends.
Inputs may be any that keep to these rules, and one draw needn't show every extreme that they name: `enc_lengths`: every document has more than half of 2048 valid positions, and at least one document is full.
All inputs are finite; a program needn't handle non-finite values.
Results may differ from the reference program's by a relative error of at most 0.012.
The reference program's roundings to bfloat16 on the way (of `keys`, `values` and `rounded`) count: a program that leaves them out, or rounds other values in their place, can miss the bound.
Values may be sent and summed in bfloat16 or wider, within the bound.
No kernel may reach another device: no remote copies, remote signals or barrier semaphores. Data moves between devices by JAX's collectives and lax.ppermute only.
A program may use at most 64 MiB of HBM per device.

```python
import math
import jax
import jax.numpy as jnp
from jax import lax

D = 4096
HEAD_DIM = 256
HEADS = 8
MICRO = 2
SECTIONS = 16
ENC_LEN = 2048
DEC = 1024
HF = 2048


def draw_queries(key, part):
    first = jax.random.fold_in(key, 0)
    base = jax.random.normal(first, (SECTIONS, MICRO, DEC, HF), jnp.float32)
    return jnp.clip(base, -240.0, 240.0).astype(jnp.bfloat16)


def draw_enc_lengths(key, part):
    first, second = jax.random.split(key)
    counts = jax.random.randint(first, (MICRO,), ENC_LEN // 2 + 1, ENC_LEN + 1)
    which = jax.random.randint(second, (), 0, MICRO)
    return jnp.where(jnp.arange(MICRO) == which, ENC_LEN, counts).astype(jnp.int32)


def steps_of(key, shape, cuts, low, high):
    loudness = 1.0
    for dim, blocks in cuts:
        heights = jax.random.uniform(jax.random.fold_in(jax.random.fold_in(key, 6), dim), (blocks,), jnp.float32, low / len(cuts), high / len(cuts))
        loudness = loudness * jnp.repeat(jnp.exp(heights), shape[dim] // blocks).reshape((-1,) + (1,) * (len(shape) - 1 - dim))
    return loudness


def normal_values(rng, shape, scale, bound, cuts=(), kind=jnp.bfloat16):
    result = jax.random.normal(rng, shape, jnp.float32) * scale
    if len(cuts) > 0:
        result = steps_of(rng, shape, cuts, -0.22, 0.18) * result
    return jnp.clip(result, min=-bound, max=bound).astype(kind)


def setup_inputs(seed: int = 0) -> dict:
    arg_keys = jax.random.split(jax.random.key(seed), 6)
    return {
        "queries": draw_queries(jax.random.fold_in(arg_keys[5], 71), 0),
        "enc_states": normal_values(arg_keys[1], (MICRO, ENC_LEN, D), 1.0, 6.0, ((1, 8), (2, 16))),
        "key_weight": normal_values(arg_keys[2], (SECTIONS, D, HF), D ** -0.5, 0.09375, ((0, 16), (1, 8), (2, 4))),
        "value_weight": normal_values(arg_keys[3], (SECTIONS, D, HF), D ** -0.5, 0.09375, ((0, 16), (1, 8), (2, 4))),
        "enc_lengths": draw_enc_lengths(jax.random.fold_in(arg_keys[5], 71), 0),
    }


def reference(queries, enc_states, key_weight, value_weight, enc_lengths):
    scale = 1.0 / math.sqrt(HEAD_DIM)
    valid = jnp.arange(ENC_LEN).astype(jnp.int32)[None, :] < enc_lengths[:, None]
    states = enc_states.astype(jnp.float32)

    def section(operands):
        query_block, w_key, w_value = operands
        keys = jnp.einsum('mld,dh->mlh', states, w_key.astype(jnp.float32), precision=lax.Precision.HIGHEST).astype(jnp.bfloat16)
        values = jnp.einsum('mld,dh->mlh', states, w_value.astype(jnp.float32), precision=lax.Precision.HIGHEST).astype(jnp.bfloat16)
        keys = lax.optimization_barrier(keys).astype(jnp.float32).reshape(MICRO, ENC_LEN, HEADS, HEAD_DIM)
        values = lax.optimization_barrier(values).astype(jnp.float32).reshape(MICRO, ENC_LEN, HEADS, HEAD_DIM)
        query_heads = query_block.astype(jnp.float32).reshape(MICRO, DEC, HEADS, HEAD_DIM)
        scores = jnp.einsum('mthd,mlhd->mhtl', query_heads, keys, precision=lax.Precision.HIGHEST) * scale
        scores = jnp.where(valid[:, None, None, :], scores, -jnp.inf)
        top = lax.optimization_barrier(jnp.max(scores, axis=-1, keepdims=True))
        weights = jnp.exp(scores - top)
        total = lax.optimization_barrier(jnp.sum(weights, axis=-1, keepdims=True))
        rounded = lax.optimization_barrier(weights.astype(jnp.bfloat16)).astype(jnp.float32)
        mixed = jnp.einsum('mhtl,mlhd->mhtd', rounded, values, precision=lax.Precision.HIGHEST) / total
        return mixed.transpose(0, 2, 1, 3).reshape(MICRO, DEC, HF).astype(jnp.bfloat16)
    return lax.map(section, (queries, key_weight, value_weight))
```

```python
import math

import jax
import jax.numpy as jnp
from jax import lax
from jax.experimental import pallas as pl
from jax.experimental.pallas import tpu as pltpu
from jax.sharding import Mesh
from jax.sharding import PartitionSpec as P

HEAD_DIM = 256
SEGMENT = ("zh", "y")
CTX = ("x", "c")
ROWS = 256
FEATS = 256
VMEM = pl.BlockSpec(memory_space=pltpu.VMEM)
SMEM = pl.BlockSpec(memory_space=pltpu.SMEM)
HBM = pl.BlockSpec(memory_space=pl.ANY)


def shift(array, axis, by):
    n = lax.axis_size(axis)
    return lax.ppermute(array, axis, [(i, (i + by) % n) for i in range(n)])


def ring_of_eight(block):
    up, down = block, block
    pieces = [block]
    for _ in range(3):
        up, down = shift(up, "y", 1), shift(down, "y", -1)
        pieces += [up, down]
    return pieces, (shift(up[0], "y", 1), shift(down[1], "y", -1))


def ring_of_four(block):
    half = block.shape[0] // 2
    right, left = shift(block, "x", 1), shift(block, "x", -1)
    return [block, right, left, shift(right[:half], "x", 1), shift(left[half:], "x", -1)]


Y_OFFSETS = (0, 7, 1, 6, 2, 5, 3)
X_OFFSETS = (0, 3, 1, 2, 2)


def store_heads(out, acc, n):
    kind, head = n // 2, n % 2
    for doc in range(2):
        out[doc * 2 + head, :, kind * HEAD_DIM : (kind + 1) * HEAD_DIM] = acc[doc * ROWS : (doc + 1) * ROWS]


def project_most_kernel(where, *refs):
    enc, own, other = refs[:7], refs[7:12], refs[12:17]
    out, w_left, enc_all, w_all, sem_e, sem_w = refs[17:]
    half, y, x, core = where[0], where[1], where[2], where[3]
    copies = []
    for side, blocks in enumerate((own, other)):
        for piece, ref in enumerate(blocks):
            block = lax.rem(x + X_OFFSETS[piece], 4)
            of_core = core if side == 0 else 1 - core
            row = block * 1024 + of_core * 512 + (256 if piece == 4 else 0)
            copies.append(
                pltpu.make_async_copy(
                    ref, w_all.at[pl.ds(pl.multiple_of(row, 256), ref.shape[0])], sem_w.at[len(copies)]
                )
            )
    halves = (half, 1 - half)
    for piece, ref in enumerate(enc):
        place = lax.rem(y + Y_OFFSETS[piece], 8)
        for near in range(2):
            column = pl.multiple_of((halves[near] * 8 + place) * FEATS, FEATS)
            copies.append(
                pltpu.make_async_copy(
                    ref.at[near], enc_all.at[:, :, pl.ds(column, FEATS)], sem_e.at[2 * piece + near]
                )
            )
    for copy in copies:
        copy.start()
    place = lax.rem(y + 4, 8)
    lefts = [pl.multiple_of((h * 8 + place) * FEATS, FEATS) for h in halves]
    for left in lefts:
        enc_all[:, :, pl.ds(left, FEATS)] = jnp.zeros((2, ROWS, FEATS), jnp.bfloat16)
    for copy in copies:
        copy.wait()
    for near in range(2):
        w_left[near] = w_all[pl.ds(lefts[near], FEATS), :]
    lhs = enc_all[...].reshape(2 * ROWS, 16 * FEATS)
    for n in range(4):
        cols = slice(n * HEAD_DIM, (n + 1) * HEAD_DIM)
        out[:, cols] = jnp.dot(lhs, w_all[:, cols], preferred_element_type=jnp.float32)


def project_most(where, enc, own, other):
    return pl.pallas_call(
        project_most_kernel,
        out_shape=(
            jax.ShapeDtypeStruct((2 * ROWS, 4 * HEAD_DIM), jnp.float32),
            jax.ShapeDtypeStruct((2, FEATS, 4 * HEAD_DIM), jnp.bfloat16),
        ),
        in_specs=[SMEM] + [HBM] * 17,
        out_specs=(VMEM, VMEM),
        scratch_shapes=[
            pltpu.VMEM((2, ROWS, 16 * FEATS), jnp.bfloat16),
            pltpu.VMEM((4096, 4 * HEAD_DIM), jnp.bfloat16),
            pltpu.SemaphoreType.DMA((14,)),
            pltpu.SemaphoreType.DMA((10,)),
        ],
        compiler_params=pltpu.CompilerParams(vmem_limit_bytes=60 * 2**20),
        cost_estimate=pl.CostEstimate(
            flops=2 * 512 * 4096 * 1024, bytes_accessed=14 * 2**20, transcendentals=0
        ),
        name="project_most",
    )(where, *enc, *own, *other)


def project_rest_kernel(near, far, partial, w_left, out):
    near_rows = near[...].reshape(2 * ROWS, FEATS)
    far_rows = far[...].reshape(2 * ROWS, FEATS)
    for n in range(4):
        cols = slice(n * HEAD_DIM, (n + 1) * HEAD_DIM)
        acc = jnp.dot(near_rows, w_left[0, :, cols], preferred_element_type=jnp.float32)
        acc += jnp.dot(far_rows, w_left[1, :, cols], preferred_element_type=jnp.float32)
        store_heads(out, (acc + partial[:, cols]).astype(jnp.bfloat16), n)


def project_rest(near, far, partial, w_left):
    return pl.pallas_call(
        project_rest_kernel,
        out_shape=jax.ShapeDtypeStruct((4, ROWS, 2 * HEAD_DIM), jnp.bfloat16),
        in_specs=[VMEM] * 4,
        out_specs=VMEM,
        compiler_params=pltpu.CompilerParams(vmem_limit_bytes=60 * 2**20),
        cost_estimate=pl.CostEstimate(
            flops=2 * 512 * 512 * 1024, bytes_accessed=5 * 2**20, transcendentals=0
        ),
        name="project_rest",
    )(near, far, partial, w_left)


def attend_kernel(where, lengths, query, mine, theirs, out):
    x, core = where[2], where[3]
    length = lengths[x // 2]
    scale = 1.0 / math.sqrt(HEAD_DIM)
    steps = [(ref, of, p) for of, ref in ((core, mine), (1 - core, theirs)) for p in range(4)]
    for chunk in range(4):
        q = query[chunk]
        scores = []
        for ref, of, p in steps:
            keys = ref[p, :, :HEAD_DIM]
            s = lax.dot_general(q, keys, (((1,), (1,)), ((), ())), preferred_element_type=jnp.float32)
            place = (p * 2 + of) * ROWS + lax.broadcasted_iota(jnp.int32, (1, ROWS), 1)
            scores.append(jnp.where(place < length, s * scale, -jnp.inf))
        top = scores[0]
        for s in scores[1:]:
            top = jnp.maximum(top, s)
        top = jnp.max(top, axis=1, keepdims=True)
        total, summed = None, None
        for s, (ref, _, p) in zip(scores, steps):
            w = jnp.exp(s - top)
            total = w if total is None else total + w
            o = jnp.dot(w.astype(jnp.bfloat16), ref[p, :, HEAD_DIM:], preferred_element_type=jnp.float32)
            summed = o if summed is None else summed + o
        total = jnp.sum(total, axis=1, keepdims=True)
        out[chunk] = (summed / total).astype(jnp.bfloat16)


def attend(where, lengths, query, mine, theirs):
    return pl.pallas_call(
        attend_kernel,
        out_shape=jax.ShapeDtypeStruct((4, 128, HEAD_DIM), jnp.bfloat16),
        in_specs=[SMEM, SMEM, VMEM, VMEM, VMEM],
        out_specs=VMEM,
        compiler_params=pltpu.CompilerParams(vmem_limit_bytes=60 * 2**20),
        cost_estimate=pl.CostEstimate(
            flops=4 * 512 * 2048 * 256, bytes_accessed=4 * 2**20, transcendentals=512 * 2048
        ),
        name="attend",
    )(where, lengths, query, mine, theirs)


def on_device(queries, enc_states, key_weight, value_weight, enc_lengths):
    zh, y = lax.axis_index("zh"), lax.axis_index("y")
    x, core = lax.axis_index("x"), lax.axis_index("c")
    where = jnp.stack([zh, y, x, core])

    far = shift(enc_states, "zh", 1)

    query = queries[0].reshape(2, 128, 2, HEAD_DIM).transpose(0, 2, 1, 3).reshape(4, 128, HEAD_DIM)
    query = lax.all_to_all(query, "x", 0, 0)

    weight = jnp.concatenate([key_weight[0], value_weight[0]], axis=1)
    weight, query = lax.optimization_barrier((weight, query))
    own = ring_of_four(weight)
    other = [shift(block, "c", 1) for block in own]
    enc, (rest_near, rest_far) = ring_of_eight(jnp.stack([enc_states, far]))

    most, w_left = project_most(where, enc, own, other)
    both = project_rest(rest_near, rest_far, most, w_left)
    mine = lax.all_to_all(both, "x", 0, 0)
    theirs = shift(mine, "c", 1)
    mixed = attend(where, enc_lengths, query, mine, theirs)
    mixed = lax.all_to_all(mixed, "x", 0, 0)
    mixed = mixed.reshape(2, 2, 128, HEAD_DIM).transpose(0, 2, 1, 3).reshape(2, 128, 2 * HEAD_DIM)
    return mixed[None]


def solution(mesh):
    torus = Mesh(mesh.devices.reshape(2, 8, 4, 2, 4), ("zh", "y", "x", "c", "mp"))
    return jax.shard_map(
        on_device,
        mesh=torus,
        in_specs=(
            P(SEGMENT, None, CTX, "mp"),
            P(None, CTX, SEGMENT),
            P(SEGMENT, CTX, "mp"),
            P(SEGMENT, CTX, "mp"),
            P(),
        ),
        out_specs=P(SEGMENT, None, CTX, "mp"),
        check_vma=False,
    )
```

```python
import math

import jax
import jax.numpy as jnp
from jax import lax
from jax.experimental import pallas as pl
from jax.experimental.pallas import tpu as pltpu
from jax.sharding import Mesh
from jax.sharding import PartitionSpec as P

HEAD_DIM = 256
SEGMENT = ("zh", "y")
X = ("xh", "xl")
CTX = ("xh", "xl", "c")
ROWS = 256
FEATS = 256
VMEM = pl.BlockSpec(memory_space=pltpu.VMEM)
SMEM = pl.BlockSpec(memory_space=pltpu.SMEM)
ANY = pl.BlockSpec(memory_space=pl.ANY)


def shift(array, axis, by):
    n = lax.axis_size(axis)
    by %= n
    return lax.ppermute(array, axis, [(i, (i + by) % n) for i in range(n)])


def ring_of_eight(block):
    up, down = block, block
    pieces = [block]
    for _ in range(3):
        up, down = shift(up, "y", 1), shift(down, "y", -1)
        pieces += [up, down]
    return pieces, (shift(up[0], "y", 1), shift(down[1], "y", -1))


X_OFFSETS = (0, 3, 1, 2)


def slot_of(relative):
    odd_even = jnp.where(relative < 4, 2 * relative, 2 * (8 - relative) - 1)
    return jnp.where(relative == 4, 7, jnp.where(relative == 0, 0, odd_even))


def project_early_kernel(where, *refs):
    enc, own, other = refs[:5], refs[5:9], refs[9:13]
    out, w_left, enc_all, w_all, sem_e, sem_w = refs[13:]
    y, x, core = where[0], where[1], where[2]
    copies = []
    for side, blocks in enumerate((own, other)):
        of_core = core if side == 0 else 1 - core
        for ref, offset in zip(blocks, X_OFFSETS):
            block = lax.rem(x + offset, 4)
            for part in range(2):
                segment = (block * 2 + of_core) * 2 + part
                relative = lax.rem(lax.rem(segment, 8) - y + 8, 8)
                row = (slot_of(relative) * 2 + block // 2) * FEATS
                copies.append(
                    pltpu.make_async_copy(
                        ref.at[pl.ds(part * FEATS, FEATS)],
                        w_all.at[pl.ds(pl.multiple_of(row, FEATS), FEATS)],
                        sem_w.at[len(copies)],
                    )
                )
    for piece, ref in enumerate(enc):
        for high in range(2):
            n = 2 * piece + high
            copies.append(
                pltpu.make_async_copy(
                    ref.at[high], enc_all.at[:, :, pl.ds(n * FEATS, FEATS)], sem_e.at[n]
                )
            )
    for copy in copies:
        copy.start()
    for copy in copies:
        copy.wait()
    depth = 2 * len(enc) * FEATS
    lhs = enc_all[...].reshape(2 * ROWS, depth)
    for n in range(4):
        cols = slice(n * HEAD_DIM, (n + 1) * HEAD_DIM)
        out[:, cols] = jnp.dot(lhs, w_all[:depth, cols], preferred_element_type=jnp.float32)
    for n in range(6):
        w_left[n] = w_all[depth + n * FEATS : depth + (n + 1) * FEATS, :]


def project_early(where, enc, own, other):
    return pl.pallas_call(
        project_early_kernel,
        out_shape=(
            jax.ShapeDtypeStruct((2 * ROWS, 4 * HEAD_DIM), jnp.float32),
            jax.ShapeDtypeStruct((6, FEATS, 4 * HEAD_DIM), jnp.bfloat16),
        ),
        in_specs=[SMEM] + [ANY] * 13,
        out_specs=(VMEM, VMEM),
        scratch_shapes=[
            pltpu.VMEM((2, ROWS, 10 * FEATS), jnp.bfloat16),
            pltpu.VMEM((4096, 4 * HEAD_DIM), jnp.bfloat16),
            pltpu.SemaphoreType.DMA((10,)),
            pltpu.SemaphoreType.DMA((16,)),
        ],
        compiler_params=pltpu.CompilerParams(vmem_limit_bytes=32 * 2**20),
        cost_estimate=pl.CostEstimate(
            flops=2 * 512 * 2560 * 1024, bytes_accessed=14 * 2**20, transcendentals=0
        ),
        name="project_early",
    )(where, *enc, *own, *other)


def project_next_kernel(up, down, partial, w_left, out):
    for n in range(4):
        cols = slice(n * HEAD_DIM, (n + 1) * HEAD_DIM)
        acc = partial[:, cols]
        for k, (ref, high) in enumerate(((up, 0), (up, 1), (down, 0), (down, 1))):
            rows = ref[high].reshape(2 * ROWS, FEATS)
            acc += jnp.dot(rows, w_left[k, :, cols], preferred_element_type=jnp.float32)
        out[:, cols] = acc


def project_next(up, down, partial, w_left):
    return pl.pallas_call(
        project_next_kernel,
        out_shape=jax.ShapeDtypeStruct((2 * ROWS, 4 * HEAD_DIM), jnp.float32),
        in_specs=[VMEM] * 4,
        out_specs=VMEM,
        compiler_params=pltpu.CompilerParams(vmem_limit_bytes=32 * 2**20),
        cost_estimate=pl.CostEstimate(
            flops=2 * 512 * 1024 * 1024, bytes_accessed=8 * 2**20, transcendentals=0
        ),
        name="project_next",
    )(up, down, partial, w_left)


def project_rest_kernel(first, second, partial, w_left, out):
    first_rows = first[...].reshape(2 * ROWS, FEATS)
    second_rows = second[...].reshape(2 * ROWS, FEATS)
    for n in range(4):
        cols = slice(n * HEAD_DIM, (n + 1) * HEAD_DIM)
        acc = jnp.dot(first_rows, w_left[4, :, cols], preferred_element_type=jnp.float32)
        acc += jnp.dot(second_rows, w_left[5, :, cols], preferred_element_type=jnp.float32)
        out[:, cols] = (acc + partial[:, cols]).astype(jnp.bfloat16)


def project_rest(first, second, partial, w_left):
    return pl.pallas_call(
        project_rest_kernel,
        out_shape=jax.ShapeDtypeStruct((2 * ROWS, 4 * HEAD_DIM), jnp.bfloat16),
        in_specs=[VMEM] * 4,
        out_specs=VMEM,
        compiler_params=pltpu.CompilerParams(vmem_limit_bytes=32 * 2**20),
        cost_estimate=pl.CostEstimate(
            flops=2 * 512 * 512 * 1024, bytes_accessed=5 * 2**20, transcendentals=0
        ),
        name="project_rest",
    )(first, second, partial, w_left)


def attend_kernel(where, lengths, query, mine, theirs, out):
    x, core = where[1], where[2]
    length = lengths[lax.rem(x, 2)]
    scale = 1.0 / math.sqrt(HEAD_DIM)
    steps = []
    for of, ref in ((core, mine), (1 - core, theirs)):
        index = lax.broadcasted_iota(jnp.int32, (1, 2 * ROWS), 1)
        first = (x // 2 * 4 + of) * ROWS
        place = index + jnp.where(index < ROWS, first, first + ROWS)
        steps.append((ref, place < length))
    lane = lax.broadcasted_iota(jnp.int32, (128, 128), 1)
    for chunk in range(2):
        tables = [jnp.zeros((128, 128), jnp.float32)] * 2
        for head in range(2):
            key_cols = slice(head * HEAD_DIM, (head + 1) * HEAD_DIM)
            value_cols = slice((2 + head) * HEAD_DIM, (3 + head) * HEAD_DIM)
            q = query[2 * chunk : 2 * chunk + 2, :, key_cols].reshape(256, HEAD_DIM)
            scores = []
            for ref, valid in steps:
                s = lax.dot_general(
                    q, ref[:, key_cols], (((1,), (1,)), ((), ())), preferred_element_type=jnp.float32
                )
                scores.append(jnp.where(valid, s * scale, -1e30))
            top = jnp.max(jnp.maximum(scores[0], scores[1]), axis=1, keepdims=True)
            weights = [jnp.exp(s - top) for s in scores]
            total = jnp.sum(weights[0] + weights[1], axis=1, keepdims=True)
            summed = sum(
                jnp.dot(w.astype(jnp.bfloat16), ref[:, value_cols], preferred_element_type=jnp.float32)
                for w, (ref, _) in zip(weights, steps)
            )
            mixed = (summed / total).astype(jnp.bfloat16)
            log_total = top + jnp.log(total)
            high = log_total.astype(jnp.bfloat16).astype(jnp.float32)
            middle = (log_total - high).astype(jnp.bfloat16).astype(jnp.float32)
            low = log_total - high - middle
            for half in range(2):
                rows = slice(half * 128, (half + 1) * 128)
                out[2 * chunk + half, :128, key_cols] = mixed[rows]
                for at, part in enumerate((high, middle, low)):
                    tables[half] = jnp.where(lane == 3 * head + at, part[rows], tables[half])
        for half in range(2):
            out[2 * chunk + half, 128:, :128] = jnp.transpose(tables[half])[:16].astype(jnp.bfloat16)
            out[2 * chunk + half, 128:, 128:] = jnp.zeros((16, 2 * HEAD_DIM - 128), jnp.bfloat16)


def attend(where, lengths, query, mine, theirs):
    return pl.pallas_call(
        attend_kernel,
        out_shape=jax.ShapeDtypeStruct((4, 144, 2 * HEAD_DIM), jnp.bfloat16),
        in_specs=[SMEM, SMEM, VMEM, VMEM, VMEM],
        out_specs=VMEM,
        compiler_params=pltpu.CompilerParams(vmem_limit_bytes=32 * 2**20),
        cost_estimate=pl.CostEstimate(
            flops=4 * 1024 * 1024 * 256, bytes_accessed=4 * 2**20, transcendentals=1024 * 1024
        ),
        name="attend",
    )(where, lengths, query, mine, theirs)


def merge_kernel(parts, out):
    for doc in range(2):
        tables = [parts[doc + 2 * xh, 128:, :128].astype(jnp.float32) for xh in range(2)]
        for head in range(2):
            cols = slice(head * HEAD_DIM, (head + 1) * HEAD_DIM)
            logs = []
            for table in tables:
                row = sum(table[3 * head + at : 3 * head + at + 1] for at in range(3))
                logs.append(jnp.transpose(jnp.broadcast_to(row, (128, 128)))[:, :1])
            top = jnp.maximum(logs[0], logs[1])
            shares = [jnp.exp(log - top) for log in logs]
            mixed = sum(
                share * parts[doc + 2 * xh, :128, cols].astype(jnp.float32) for xh, share in enumerate(shares)
            )
            out[0, doc, :, cols] = (mixed / (shares[0] + shares[1])).astype(jnp.bfloat16)


def merge(parts):
    return pl.pallas_call(
        merge_kernel,
        out_shape=jax.ShapeDtypeStruct((1, 2, 128, 2 * HEAD_DIM), jnp.bfloat16),
        in_specs=[VMEM],
        out_specs=VMEM,
        name="merge",
    )(parts)


def on_device(queries, enc_states, key_weight, value_weight, enc_lengths):
    x = lax.axis_index("xh") * 2 + lax.axis_index("xl")
    where = jnp.stack([lax.axis_index("y"), x, lax.axis_index("c")])

    states = jnp.broadcast_to(enc_states[None], (2, *enc_states.shape)).reshape(4, ROWS, FEATS)
    states = lax.all_to_all(states, ("zh", "xl"), 0, 0).reshape(2, 2, ROWS, FEATS)

    weight = jnp.concatenate([key_weight[0], value_weight[0]], axis=1)
    late, states = lax.optimization_barrier((weight, states))
    own = [weight, shift(weight, X, 1), shift(weight, X, -1), shift(late, X, 2)]
    other = [shift(block, "c", 1) for block in own]
    enc, (first, second) = ring_of_eight(states)

    query = jnp.broadcast_to(queries, (2, *queries.shape[1:])).reshape(4, *queries.shape[2:])
    query, own[3] = lax.optimization_barrier((query, own[3]))
    query = lax.all_to_all(query, X, 0, 0)

    partial, w_left = project_early(where, enc[:5], own, other)
    partial = project_next(enc[5], enc[6], partial, w_left)
    mine = project_rest(first, second, partial, w_left)
    mine, query = lax.optimization_barrier((mine, query))
    theirs = shift(mine, "c", 1)
    parts = attend(where, enc_lengths, query, mine, theirs)
    return merge(lax.all_to_all(parts, X, 0, 0))


def solution(mesh):
    torus = Mesh(mesh.devices.reshape(2, 8, 2, 2, 2, 4), ("zh", "y", "xh", "xl", "c", "mp"))
    return jax.shard_map(
        on_device,
        mesh=torus,
        in_specs=(
            P(SEGMENT, None, CTX, "mp"),
            P(None, CTX, SEGMENT),
            P(SEGMENT, CTX, "mp"),
            P(SEGMENT, CTX, "mp"),
            P(),
        ),
        out_specs=P(SEGMENT, None, CTX, "mp"),
        check_vma=False,
    )
```

```python
import math

import jax
import jax.numpy as jnp
from jax import lax
from jax.experimental import pallas as pl
from jax.experimental.pallas import tpu as pltpu
from jax.sharding import Mesh
from jax.sharding import PartitionSpec as P

HEAD_DIM = 256
SEGMENT = ("zh", "y")
CTX = ("x", "c")
ROWS = 256
FEATS = 256
VMEM = pl.BlockSpec(memory_space=pltpu.VMEM)
SMEM = pl.BlockSpec(memory_space=pltpu.SMEM)
ANY = pl.BlockSpec(memory_space=pl.ANY)


def shift(array, axis, by):
    n = lax.axis_size(axis)
    return lax.ppermute(array, axis, [(i, (i + by) % n) for i in range(n)])


def ring_of_eight(block):
    up, down = block, block
    pieces = [block]
    for _ in range(3):
        up, down = shift(up, "y", 1), shift(down, "y", -1)
        pieces += [up, down]
    return pieces, (shift(up[0], "y", 1), shift(down[1], "y", -1))


def ring_of_four(block):
    half = block.shape[0] // 2
    right, left = shift(block, "x", 1), shift(block, "x", -1)
    return [block, right, left, shift(right[:half], "x", 1), shift(left[half:], "x", -1)]


X_OFFSETS = (0, 3, 1, 2, 2)


def slot_of(relative):
    odd_even = jnp.where(relative < 4, 2 * relative, 2 * (8 - relative) - 1)
    return jnp.where(relative == 4, 7, jnp.where(relative == 0, 0, odd_even))


def store_heads(out, acc, n):
    kind, head = n // 2, n % 2
    for doc in range(2):
        out[doc * 2 + head, :ROWS, kind * HEAD_DIM : (kind + 1) * HEAD_DIM] = acc[doc * ROWS : (doc + 1) * ROWS]


def project_most_kernel(where, *refs):
    enc, own, other = refs[:7], refs[7:12], refs[12:17]
    out, w_left, enc_all, w_all, sem_e, sem_w = refs[17:]
    y, x, core = where[0], where[1], where[2]
    parts = []
    for side, blocks in enumerate((own, other)):
        of_core = core if side == 0 else 1 - core
        for piece, ref in enumerate(blocks):
            block = lax.rem(x + X_OFFSETS[piece], 4)
            for part in range(ref.shape[0] // FEATS):
                within = 1 if piece == 4 else part
                segment = (block * 2 + of_core) * 2 + within
                relative = lax.rem(lax.rem(segment, 8) - y + 8, 8)
                row = (slot_of(relative) * 2 + segment // 8) * FEATS
                parts.append((ref, part * FEATS, pl.multiple_of(row, FEATS)))
    enc_copies = [
        pltpu.make_async_copy(
            ref.at[high],
            enc_all.at[:, :, pl.ds((2 * piece + high) * FEATS, FEATS)],
            sem_e.at[2 * piece + high],
        )
        for piece, ref in enumerate(enc)
        for high in range(2)
    ]
    half = 2 * HEAD_DIM
    w_copies = [
        [
            pltpu.make_async_copy(
                ref.at[pl.ds(start, FEATS), pl.ds(kind * half, half)],
                w_all.at[pl.ds(row, FEATS), pl.ds(kind * half, half)],
                sem_w.at[kind, n],
            )
            for n, (ref, start, row) in enumerate(parts)
        ]
        for kind in range(2)
    ]
    for copy in enc_copies + w_copies[0] + w_copies[1]:
        copy.start()
    for copy in enc_copies:
        copy.wait()
    depth = 2 * len(enc) * FEATS
    lhs = enc_all[...].reshape(2 * ROWS, depth)
    for kind in range(2):
        for copy in w_copies[kind]:
            copy.wait()
        for head in range(2):
            n = 2 * kind + head
            cols = slice(n * HEAD_DIM, (n + 1) * HEAD_DIM)
            out[:, cols] = jnp.dot(lhs, w_all[:depth, cols], preferred_element_type=jnp.float32)
    for high in range(2):
        w_left[high] = w_all[depth + high * FEATS : depth + (high + 1) * FEATS, :]


def project_most(where, enc, own, other):
    return pl.pallas_call(
        project_most_kernel,
        out_shape=(
            jax.ShapeDtypeStruct((2 * ROWS, 4 * HEAD_DIM), jnp.float32),
            jax.ShapeDtypeStruct((2, FEATS, 4 * HEAD_DIM), jnp.bfloat16),
        ),
        in_specs=[SMEM] + [ANY] * 17,
        out_specs=(VMEM, VMEM),
        scratch_shapes=[
            pltpu.VMEM((2, ROWS, 14 * FEATS), jnp.bfloat16),
            pltpu.VMEM((4096, 4 * HEAD_DIM), jnp.bfloat16),
            pltpu.SemaphoreType.DMA((14,)),
            pltpu.SemaphoreType.DMA((2, 16)),
        ],
        compiler_params=pltpu.CompilerParams(vmem_limit_bytes=32 * 2**20),
        cost_estimate=pl.CostEstimate(
            flops=2 * 512 * 3584 * 1024, bytes_accessed=14 * 2**20, transcendentals=0
        ),
        name="project_most",
    )(where, *enc, *own, *other)


def project_rest_kernel(first, second, partial, w_left, queries, out):
    first_rows = first[...].reshape(2 * ROWS, FEATS)
    second_rows = second[...].reshape(2 * ROWS, FEATS)
    for n in range(4):
        cols = slice(n * HEAD_DIM, (n + 1) * HEAD_DIM)
        acc = jnp.dot(first_rows, w_left[0, :, cols], preferred_element_type=jnp.float32)
        acc += jnp.dot(second_rows, w_left[1, :, cols], preferred_element_type=jnp.float32)
        store_heads(out, (acc + partial[:, cols]).astype(jnp.bfloat16), n)
    for doc in range(2):
        for head in range(2):
            cols = slice(head * HEAD_DIM, (head + 1) * HEAD_DIM)
            for part in range(2):
                out[doc * 2 + head, ROWS:, part * HEAD_DIM : (part + 1) * HEAD_DIM] = queries[
                    0, doc, part * 64 : (part + 1) * 64, cols
                ]


def project_rest(first, second, partial, w_left, queries):
    return pl.pallas_call(
        project_rest_kernel,
        out_shape=jax.ShapeDtypeStruct((4, ROWS + 64, 2 * HEAD_DIM), jnp.bfloat16),
        in_specs=[VMEM] * 5,
        out_specs=VMEM,
        compiler_params=pltpu.CompilerParams(vmem_limit_bytes=32 * 2**20),
        cost_estimate=pl.CostEstimate(
            flops=2 * 512 * 512 * 1024, bytes_accessed=5 * 2**20, transcendentals=0
        ),
        name="project_rest",
    )(first, second, partial, w_left, queries)


def attend_kernel(where, lengths, mine, theirs, out):
    x, core = where[1], where[2]
    length = lengths[x // 2]
    scale = 1.0 / math.sqrt(HEAD_DIM)
    steps = [(ref, of, p) for of, ref in ((core, mine), (1 - core, theirs)) for p in range(4)]
    for chunk in range(4):
        q = jnp.concatenate([mine[chunk, ROWS:, :HEAD_DIM], mine[chunk, ROWS:, HEAD_DIM:]], axis=0)
        scores = []
        for ref, of, p in steps:
            keys = ref[p, :ROWS, :HEAD_DIM]
            s = lax.dot_general(q, keys, (((1,), (1,)), ((), ())), preferred_element_type=jnp.float32)
            place = (p * 2 + of) * ROWS + lax.broadcasted_iota(jnp.int32, (1, ROWS), 1)
            scores.append(jnp.where(place < length, s * scale, -jnp.inf))
        top = scores[0]
        for s in scores[1:]:
            top = jnp.maximum(top, s)
        top = jnp.max(top, axis=1, keepdims=True)
        total, summed = None, None
        for s, (ref, _, p) in zip(scores, steps):
            w = jnp.exp(s - top)
            total = w if total is None else total + w
            o = jnp.dot(w.astype(jnp.bfloat16), ref[p, :ROWS, HEAD_DIM:], preferred_element_type=jnp.float32)
            summed = o if summed is None else summed + o
        total = jnp.sum(total, axis=1, keepdims=True)
        out[chunk] = (summed / total).astype(jnp.bfloat16)


def attend(where, lengths, mine, theirs):
    return pl.pallas_call(
        attend_kernel,
        out_shape=jax.ShapeDtypeStruct((4, 128, HEAD_DIM), jnp.bfloat16),
        in_specs=[SMEM, SMEM, VMEM, VMEM],
        out_specs=VMEM,
        compiler_params=pltpu.CompilerParams(vmem_limit_bytes=32 * 2**20),
        cost_estimate=pl.CostEstimate(
            flops=4 * 512 * 2048 * 256, bytes_accessed=4 * 2**20, transcendentals=512 * 2048
        ),
        name="attend",
    )(where, lengths, mine, theirs)


def on_device(queries, enc_states, key_weight, value_weight, enc_lengths):
    where = jnp.stack([lax.axis_index("y"), lax.axis_index("x"), lax.axis_index("c")])
    weight = jnp.concatenate([key_weight[0], value_weight[0]], axis=1)
    own = ring_of_four(weight)
    other = [shift(block, "c", 1) for block in own]
    enc, (first, second) = ring_of_eight(lax.all_gather(enc_states, "zh"))

    partial, w_left = project_most(where, enc, own, other)
    both = project_rest(first, second, partial, w_left, queries)
    mine = lax.all_to_all(both, "x", 0, 0)
    theirs = shift(mine, "c", 1)
    mixed = attend(where, enc_lengths, mine, theirs)
    mixed = lax.all_to_all(mixed, "x", 0, 0)
    mixed = mixed.reshape(2, 2, 128, HEAD_DIM).transpose(0, 2, 1, 3).reshape(2, 128, 2 * HEAD_DIM)
    return mixed[None]


def solution(mesh):
    torus = Mesh(mesh.devices.reshape(2, 8, 4, 2, 4), ("zh", "y", "x", "c", "mp"))
    return jax.shard_map(
        on_device,
        mesh=torus,
        in_specs=(
            P(SEGMENT, None, CTX, "mp"),
            P(None, CTX, SEGMENT),
            P(SEGMENT, CTX, "mp"),
            P(SEGMENT, CTX, "mp"),
            P(),
        ),
        out_specs=P(SEGMENT, None, CTX, "mp"),
        check_vma=False,
    )
```

```python
import math

import jax
import jax.numpy as jnp
from jax import lax
from jax.experimental import pallas as pl
from jax.experimental.pallas import tpu as pltpu
from jax.sharding import Mesh
from jax.sharding import PartitionSpec as P

HEAD_DIM = 256
SEGMENT = ("zh", "y")
CTX = ("x", "c")
ROWS = 256
FEATS = 256
VMEM = pl.BlockSpec(memory_space=pltpu.VMEM)
SMEM = pl.BlockSpec(memory_space=pltpu.SMEM)
ANY = pl.BlockSpec(memory_space=pl.ANY)


def shift(array, axis, by):
    n = lax.axis_size(axis)
    return lax.ppermute(array, axis, [(i, (i + by) % n) for i in range(n)])


def in_hbm(array):
    return pltpu.with_memory_space_constraint(array, pltpu.HBM)


def ring_of_eight(block):
    up, down = block, block
    pieces = [block]
    for _ in range(3):
        up, down = shift(up, "y", 1), shift(down, "y", -1)
        pieces += [up, down]
    return pieces, (shift(up[0], "y", 1), shift(down[1], "y", -1))


def ring_of_four(block):
    half = block.shape[0] // 2
    right, left = shift(block, "x", 1), shift(block, "x", -1)
    return [block, right, left, shift(right[:half], "x", 1), shift(left[half:], "x", -1)]


X_OFFSETS = (0, 3, 1, 2, 2)


def slot_of(relative):
    odd_even = jnp.where(relative < 4, 2 * relative, 2 * (8 - relative) - 1)
    return jnp.where(relative == 4, 7, jnp.where(relative == 0, 0, odd_even))


def store_heads(out, acc, n):
    kind, head = n // 2, n % 2
    for doc in range(2):
        out[doc * 2 + head, :ROWS, kind * HEAD_DIM : (kind + 1) * HEAD_DIM] = acc[doc * ROWS : (doc + 1) * ROWS]


def project_most_kernel(where, *refs):
    enc, own, other = refs[:7], refs[7:12], refs[12:17]
    out, w_left, enc_all, w_all, sem_e, sem_w = refs[17:]
    y, x, core = where[0], where[1], where[2]
    parts = []
    for side, blocks in enumerate((own, other)):
        of_core = core if side == 0 else 1 - core
        for piece, ref in enumerate(blocks):
            block = lax.rem(x + X_OFFSETS[piece], 4)
            for part in range(ref.shape[0] // FEATS):
                within = 1 if piece == 4 else part
                segment = (block * 2 + of_core) * 2 + within
                relative = lax.rem(lax.rem(segment, 8) - y + 8, 8)
                row = (slot_of(relative) * 2 + segment // 8) * FEATS
                parts.append((ref, part * FEATS, pl.multiple_of(row, FEATS)))
    enc_copies = [
        pltpu.make_async_copy(
            ref.at[high],
            enc_all.at[:, :, pl.ds((2 * piece + high) * FEATS, FEATS)],
            sem_e.at[2 * piece + high],
        )
        for piece, ref in enumerate(enc)
        for high in range(2)
    ]
    half = 2 * HEAD_DIM
    w_copies = [
        [
            pltpu.make_async_copy(
                ref.at[pl.ds(start, FEATS), pl.ds(kind * half, half)],
                w_all.at[pl.ds(row, FEATS), pl.ds(kind * half, half)],
                sem_w.at[kind, n],
            )
            for n, (ref, start, row) in enumerate(parts)
        ]
        for kind in range(2)
    ]
    for copy in enc_copies + w_copies[0] + w_copies[1]:
        copy.start()
    for copy in enc_copies:
        copy.wait()
    depth = 2 * len(enc) * FEATS
    lhs = enc_all[...].reshape(2 * ROWS, depth)
    for kind in range(2):
        for copy in w_copies[kind]:
            copy.wait()
        for head in range(2):
            n = 2 * kind + head
            cols = slice(n * HEAD_DIM, (n + 1) * HEAD_DIM)
            out[:, cols] = jnp.dot(lhs, w_all[:depth, cols], preferred_element_type=jnp.float32)
    for high in range(2):
        w_left[high] = w_all[depth + high * FEATS : depth + (high + 1) * FEATS, :]


def project_most(where, enc, own, other):
    return pl.pallas_call(
        project_most_kernel,
        out_shape=(
            jax.ShapeDtypeStruct((2 * ROWS, 4 * HEAD_DIM), jnp.float32),
            jax.ShapeDtypeStruct((2, FEATS, 4 * HEAD_DIM), jnp.bfloat16),
        ),
        in_specs=[SMEM] + [ANY] * 17,
        out_specs=(VMEM, VMEM),
        scratch_shapes=[
            pltpu.VMEM((2, ROWS, 14 * FEATS), jnp.bfloat16),
            pltpu.VMEM((4096, 4 * HEAD_DIM), jnp.bfloat16),
            pltpu.SemaphoreType.DMA((14,)),
            pltpu.SemaphoreType.DMA((2, 16)),
        ],
        compiler_params=pltpu.CompilerParams(vmem_limit_bytes=32 * 2**20),
        cost_estimate=pl.CostEstimate(
            flops=2 * 512 * 3584 * 1024, bytes_accessed=14 * 2**20, transcendentals=0
        ),
        name="project_most",
    )(where, *enc, *own, *other)


def project_rest_kernel(first, second, partial, w_left, queries, out):
    first_rows = first[...].reshape(2 * ROWS, FEATS)
    second_rows = second[...].reshape(2 * ROWS, FEATS)
    for n in range(4):
        cols = slice(n * HEAD_DIM, (n + 1) * HEAD_DIM)
        acc = jnp.dot(first_rows, w_left[0, :, cols], preferred_element_type=jnp.float32)
        acc += jnp.dot(second_rows, w_left[1, :, cols], preferred_element_type=jnp.float32)
        store_heads(out, (acc + partial[:, cols]).astype(jnp.bfloat16), n)
    for doc in range(2):
        for head in range(2):
            cols = slice(head * HEAD_DIM, (head + 1) * HEAD_DIM)
            for part in range(2):
                out[doc * 2 + head, ROWS:, part * HEAD_DIM : (part + 1) * HEAD_DIM] = queries[
                    0, doc, part * 64 : (part + 1) * 64, cols
                ]


def project_rest(first, second, partial, w_left, queries):
    return pl.pallas_call(
        project_rest_kernel,
        out_shape=jax.ShapeDtypeStruct((4, ROWS + 64, 2 * HEAD_DIM), jnp.bfloat16),
        in_specs=[VMEM] * 5,
        out_specs=VMEM,
        compiler_params=pltpu.CompilerParams(vmem_limit_bytes=32 * 2**20),
        cost_estimate=pl.CostEstimate(
            flops=2 * 512 * 512 * 1024, bytes_accessed=5 * 2**20, transcendentals=0
        ),
        name="project_rest",
    )(first, second, partial, w_left, queries)


def attend_kernel(where, lengths, mine, theirs, out):
    x, core = where[1], where[2]
    length = lengths[x // 2]
    scale = 1.0 / math.sqrt(HEAD_DIM)
    steps = [(ref, of, p) for of, ref in ((core, mine), (1 - core, theirs)) for p in range(4)]
    for chunk in range(4):
        q = jnp.concatenate([mine[chunk, ROWS:, :HEAD_DIM], mine[chunk, ROWS:, HEAD_DIM:]], axis=0)
        scores = []
        for ref, of, p in steps:
            keys = ref[p, :ROWS, :HEAD_DIM]
            s = lax.dot_general(q, keys, (((1,), (1,)), ((), ())), preferred_element_type=jnp.float32)
            place = (p * 2 + of) * ROWS + lax.broadcasted_iota(jnp.int32, (1, ROWS), 1)
            scores.append(jnp.where(place < length, s * scale, -jnp.inf))
        top = scores[0]
        for s in scores[1:]:
            top = jnp.maximum(top, s)
        top = jnp.max(top, axis=1, keepdims=True)
        total, summed = None, None
        for s, (ref, _, p) in zip(scores, steps):
            w = jnp.exp(s - top)
            total = w if total is None else total + w
            o = jnp.dot(w.astype(jnp.bfloat16), ref[p, :ROWS, HEAD_DIM:], preferred_element_type=jnp.float32)
            summed = o if summed is None else summed + o
        total = jnp.sum(total, axis=1, keepdims=True)
        out[chunk] = (summed / total).astype(jnp.bfloat16)


def attend(where, lengths, mine, theirs):
    return pl.pallas_call(
        attend_kernel,
        out_shape=jax.ShapeDtypeStruct((4, 128, HEAD_DIM), jnp.bfloat16),
        in_specs=[SMEM, SMEM, VMEM, VMEM],
        out_specs=VMEM,
        compiler_params=pltpu.CompilerParams(vmem_limit_bytes=32 * 2**20),
        cost_estimate=pl.CostEstimate(
            flops=4 * 512 * 2048 * 256, bytes_accessed=4 * 2**20, transcendentals=512 * 2048
        ),
        name="attend",
    )(where, lengths, mine, theirs)


def on_device(queries, enc_states, key_weight, value_weight, enc_lengths):
    where = jnp.stack([lax.axis_index("y"), lax.axis_index("x"), lax.axis_index("c")])
    weight = jnp.concatenate([key_weight[0], value_weight[0]], axis=1)
    own = ring_of_four(weight)
    other = [shift(block, "c", 1) for block in own]
    enc, (first, second) = ring_of_eight(lax.all_gather(enc_states, "zh"))

    enc[1], enc[2] = in_hbm(enc[1]), in_hbm(enc[2])
    own = own[:3] + [in_hbm(own[3]), in_hbm(own[4])]
    partial, w_left = project_most(where, enc, own, other)
    both = project_rest(first, second, partial, w_left, queries)
    mine = lax.all_to_all(both, "x", 0, 0)
    theirs = shift(mine, "c", 1)
    mixed = attend(where, enc_lengths, mine, theirs)
    mixed = lax.all_to_all(mixed, "x", 0, 0)
    mixed = mixed.reshape(2, 2, 128, HEAD_DIM).transpose(0, 2, 1, 3).reshape(2, 128, 2 * HEAD_DIM)
    return mixed[None]


def solution(mesh):
    torus = Mesh(mesh.devices.reshape(2, 8, 4, 2, 4), ("zh", "y", "x", "c", "mp"))
    return jax.shard_map(
        on_device,
        mesh=torus,
        in_specs=(
            P(SEGMENT, None, CTX, "mp"),
            P(None, CTX, SEGMENT),
            P(SEGMENT, CTX, "mp"),
            P(SEGMENT, CTX, "mp"),
            P(),
        ),
        out_specs=P(SEGMENT, None, CTX, "mp"),
        check_vma=False,
    )
```

```python
import math

import jax
import jax.numpy as jnp
from jax import lax
from jax.experimental import pallas as pl
from jax.experimental.pallas import tpu as pltpu
from jax.sharding import Mesh
from jax.sharding import PartitionSpec as P

HEAD_DIM = 256
SEGMENT = ("zh", "y")
CTX = ("x", "c")
ROWS = 256
FEATS = 256
VMEM = pl.BlockSpec(memory_space=pltpu.VMEM)
SMEM = pl.BlockSpec(memory_space=pltpu.SMEM)
ANY = pl.BlockSpec(memory_space=pl.ANY)


def shift(array, axis, by):
    n = lax.axis_size(axis)
    return lax.ppermute(array, axis, [(i, (i + by) % n) for i in range(n)])


def in_hbm(array):
    return pltpu.with_memory_space_constraint(array, pltpu.HBM)


def ring_of_eight(block):
    up, down = block, block
    pieces = [block]
    for _ in range(3):
        up, down = shift(up, "y", 1), shift(down, "y", -1)
        pieces += [up, down]
    return pieces, (shift(up[0], "y", 1), shift(down[1], "y", -1))


def ring_of_four(block):
    half = block.shape[0] // 2
    right, left = shift(block, "x", 1), shift(block, "x", -1)
    return [block, right, left, shift(right[:half], "x", 1), shift(left[half:], "x", -1)]


X_OFFSETS = (0, 3, 1, 2, 2)


def slot_of(relative):
    odd_even = jnp.where(relative < 4, 2 * relative, 2 * (8 - relative) - 1)
    return jnp.where(relative == 4, 7, jnp.where(relative == 0, 0, odd_even))


def store_heads(out, acc, n):
    kind, head = n // 2, n % 2
    for doc in range(2):
        out[doc * 2 + head, :ROWS, kind * HEAD_DIM : (kind + 1) * HEAD_DIM] = acc[doc * ROWS : (doc + 1) * ROWS]


def project_most_kernel(where, *refs):
    enc, own, other = refs[:7], refs[7:12], refs[12:17]
    out, w_left, enc_all, w_all, sem_e, sem_w = refs[17:]
    y, x, core = where[0], where[1], where[2]
    parts = []
    for side, blocks in enumerate((own, other)):
        of_core = core if side == 0 else 1 - core
        for piece, ref in enumerate(blocks):
            block = lax.rem(x + X_OFFSETS[piece], 4)
            for part in range(ref.shape[0] // FEATS):
                within = 1 if piece == 4 else part
                segment = (block * 2 + of_core) * 2 + within
                relative = lax.rem(lax.rem(segment, 8) - y + 8, 8)
                row = (slot_of(relative) * 2 + segment // 8) * FEATS
                parts.append((ref, part * FEATS, pl.multiple_of(row, FEATS)))
    enc_copies = [
        pltpu.make_async_copy(
            ref.at[high],
            enc_all.at[:, :, pl.ds((2 * piece + high) * FEATS, FEATS)],
            sem_e.at[2 * piece + high],
        )
        for piece, ref in enumerate(enc)
        for high in range(2)
    ]
    half = 2 * HEAD_DIM
    w_copies = [
        [
            pltpu.make_async_copy(
                ref.at[pl.ds(start, FEATS), pl.ds(kind * half, half)],
                w_all.at[pl.ds(row, FEATS), pl.ds(kind * half, half)],
                sem_w.at[kind, n],
            )
            for n, (ref, start, row) in enumerate(parts)
        ]
        for kind in range(2)
    ]
    for copy in enc_copies + w_copies[0] + w_copies[1]:
        copy.start()
    for copy in enc_copies:
        copy.wait()
    depth = 2 * len(enc) * FEATS
    lhs = enc_all[...].reshape(2 * ROWS, depth)
    for kind in range(2):
        for copy in w_copies[kind]:
            copy.wait()
        for head in range(2):
            n = 2 * kind + head
            cols = slice(n * HEAD_DIM, (n + 1) * HEAD_DIM)
            out[:, cols] = jnp.dot(lhs, w_all[:depth, cols], preferred_element_type=jnp.float32)
    for high in range(2):
        w_left[high] = w_all[depth + high * FEATS : depth + (high + 1) * FEATS, :]


def project_most(where, enc, own, other):
    return pl.pallas_call(
        project_most_kernel,
        out_shape=(
            jax.ShapeDtypeStruct((2 * ROWS, 4 * HEAD_DIM), jnp.float32),
            jax.ShapeDtypeStruct((2, FEATS, 4 * HEAD_DIM), jnp.bfloat16),
        ),
        in_specs=[SMEM] + [ANY] * 17,
        out_specs=(VMEM, VMEM),
        scratch_shapes=[
            pltpu.VMEM((2, ROWS, 14 * FEATS), jnp.bfloat16),
            pltpu.VMEM((4096, 4 * HEAD_DIM), jnp.bfloat16),
            pltpu.SemaphoreType.DMA((14,)),
            pltpu.SemaphoreType.DMA((2, 16)),
        ],
        compiler_params=pltpu.CompilerParams(vmem_limit_bytes=32 * 2**20),
        cost_estimate=pl.CostEstimate(
            flops=2 * 512 * 3584 * 1024, bytes_accessed=14 * 2**20, transcendentals=0
        ),
        name="project_most",
    )(where, *enc, *own, *other)


def project_rest_kernel(first, second, partial, w_left, queries, out):
    first_rows = first[...].reshape(2 * ROWS, FEATS)
    second_rows = second[...].reshape(2 * ROWS, FEATS)
    for n in range(4):
        cols = slice(n * HEAD_DIM, (n + 1) * HEAD_DIM)
        acc = jnp.dot(first_rows, w_left[0, :, cols], preferred_element_type=jnp.float32)
        acc += jnp.dot(second_rows, w_left[1, :, cols], preferred_element_type=jnp.float32)
        store_heads(out, (acc + partial[:, cols]).astype(jnp.bfloat16), n)
    for doc in range(2):
        for head in range(2):
            cols = slice(head * HEAD_DIM, (head + 1) * HEAD_DIM)
            for part in range(2):
                out[doc * 2 + head, ROWS:, part * HEAD_DIM : (part + 1) * HEAD_DIM] = queries[
                    0, doc, part * 64 : (part + 1) * 64, cols
                ]


def project_rest(first, second, partial, w_left, queries):
    return pl.pallas_call(
        project_rest_kernel,
        out_shape=jax.ShapeDtypeStruct((4, ROWS + 64, 2 * HEAD_DIM), jnp.bfloat16),
        in_specs=[VMEM] * 5,
        out_specs=VMEM,
        compiler_params=pltpu.CompilerParams(vmem_limit_bytes=32 * 2**20),
        cost_estimate=pl.CostEstimate(
            flops=2 * 512 * 512 * 1024, bytes_accessed=5 * 2**20, transcendentals=0
        ),
        name="project_rest",
    )(first, second, partial, w_left, queries)


def attend_half(where, lengths, ref, of, q):
    length = lengths[where[1] // 2]
    scores = []
    for p in range(4):
        s = lax.dot_general(
            q, ref[p, :ROWS, :HEAD_DIM], (((1,), (1,)), ((), ())), preferred_element_type=jnp.float32
        )
        place = (p * 2 + of) * ROWS + lax.broadcasted_iota(jnp.int32, (1, ROWS), 1)
        scores.append(jnp.where(place < length, s * (1.0 / math.sqrt(HEAD_DIM)), -jnp.inf))
    top = jnp.maximum(jnp.maximum(scores[0], scores[1]), jnp.maximum(scores[2], scores[3]))
    top = jnp.max(top, axis=1, keepdims=True)
    total, summed = None, None
    for p, s in enumerate(scores):
        w = jnp.exp(s - top)
        total = w if total is None else total + w
        o = jnp.dot(w.astype(jnp.bfloat16), ref[p, :ROWS, HEAD_DIM:], preferred_element_type=jnp.float32)
        summed = o if summed is None else summed + o
    return top, jnp.sum(total, axis=1, keepdims=True), summed


def query_of(mine, chunk):
    return jnp.concatenate([mine[chunk, ROWS:, :HEAD_DIM], mine[chunk, ROWS:, HEAD_DIM:]], axis=0)


def attend_mine_kernel(where, lengths, mine, top, total, summed):
    for chunk in range(4):
        t, n, o = attend_half(where, lengths, mine, where[2], query_of(mine, chunk))
        top[chunk] = jnp.broadcast_to(t, (128, 128))
        total[chunk] = jnp.broadcast_to(n, (128, 128))
        summed[chunk] = o


def attend_theirs_kernel(where, lengths, mine, theirs, top, total, summed, out):
    for chunk in range(4):
        t, n, o = attend_half(where, lengths, theirs, 1 - where[2], query_of(mine, chunk))
        before = top[chunk][:, :1]
        both = jnp.maximum(before, t)
        old, new = jnp.exp(before - both), jnp.exp(t - both)
        out[chunk] = ((old * summed[chunk] + new * o) / (old * total[chunk][:, :1] + new * n)).astype(jnp.bfloat16)


def attend(where, lengths, mine, theirs):
    cost = pl.CostEstimate(flops=2 * 512 * 2048 * 256, bytes_accessed=2 * 2**20, transcendentals=512 * 1024)
    params = pltpu.CompilerParams(vmem_limit_bytes=32 * 2**20)
    stat = jax.ShapeDtypeStruct((4, 128, 128), jnp.float32)
    state = pl.pallas_call(
        attend_mine_kernel,
        out_shape=(stat, stat, jax.ShapeDtypeStruct((4, 128, HEAD_DIM), jnp.float32)),
        in_specs=[SMEM, SMEM, VMEM],
        out_specs=(VMEM, VMEM, VMEM),
        compiler_params=params,
        cost_estimate=cost,
        name="attend_mine",
    )(where, lengths, mine)
    return pl.pallas_call(
        attend_theirs_kernel,
        out_shape=jax.ShapeDtypeStruct((4, 128, HEAD_DIM), jnp.bfloat16),
        in_specs=[SMEM, SMEM] + [VMEM] * 5,
        out_specs=VMEM,
        compiler_params=params,
        cost_estimate=cost,
        name="attend_theirs",
    )(where, lengths, mine, theirs, *state)


def on_device(queries, enc_states, key_weight, value_weight, enc_lengths):
    where = jnp.stack([lax.axis_index("y"), lax.axis_index("x"), lax.axis_index("c")])
    weight = jnp.concatenate([key_weight[0], value_weight[0]], axis=1)
    own = ring_of_four(weight)
    other = [shift(block, "c", 1) for block in own]
    enc, (first, second) = ring_of_eight(lax.all_gather(enc_states, "zh"))

    enc[1], enc[2] = in_hbm(enc[1]), in_hbm(enc[2])
    own = own[:3] + [in_hbm(own[3]), in_hbm(own[4])]
    partial, w_left = project_most(where, enc, own, other)
    both = project_rest(first, second, partial, w_left, queries)
    mine = lax.all_to_all(both, "x", 0, 0)
    theirs = shift(mine, "c", 1)
    mixed = attend(where, enc_lengths, mine, theirs)
    mixed = lax.all_to_all(mixed, "x", 0, 0)
    mixed = mixed.reshape(2, 2, 128, HEAD_DIM).transpose(0, 2, 1, 3).reshape(2, 128, 2 * HEAD_DIM)
    return mixed[None]


def solution(mesh):
    torus = Mesh(mesh.devices.reshape(2, 8, 4, 2, 4), ("zh", "y", "x", "c", "mp"))
    return jax.shard_map(
        on_device,
        mesh=torus,
        in_specs=(
            P(SEGMENT, None, CTX, "mp"),
            P(None, CTX, SEGMENT),
            P(SEGMENT, CTX, "mp"),
            P(SEGMENT, CTX, "mp"),
            P(),
        ),
        out_specs=P(SEGMENT, None, CTX, "mp"),
        check_vma=False,
    )
```

```python
import math

import jax
import jax.numpy as jnp
from jax import lax
from jax.experimental import pallas as pl
from jax.experimental.pallas import tpu as pltpu
from jax.sharding import Mesh
from jax.sharding import PartitionSpec as P

HEAD_DIM = 256
SEGMENT = ("zh", "y")
CTX = ("x", "c")
ROWS = 256
FEATS = 256
VMEM = pl.BlockSpec(memory_space=pltpu.VMEM)
SMEM = pl.BlockSpec(memory_space=pltpu.SMEM)
ANY = pl.BlockSpec(memory_space=pl.ANY)


def shift(array, axis, by):
    n = lax.axis_size(axis)
    return lax.ppermute(array, axis, [(i, (i + by) % n) for i in range(n)])


def in_hbm(array):
    return pltpu.with_memory_space_constraint(array, pltpu.HBM)


def ring_of_eight(block):
    up, down = block, block
    pieces = [block]
    for _ in range(3):
        up, down = shift(up, "y", 1), shift(down, "y", -1)
        pieces += [up, down]
    return pieces, (shift(up[0], "y", 1), shift(down[1], "y", -1))


def ring_of_four(block):
    half = block.shape[0] // 2
    right, left = shift(block, "x", 1), shift(block, "x", -1)
    return [block, right, left, shift(right[:half], "x", 1), shift(left[half:], "x", -1)]


X_OFFSETS = (0, 3, 1, 2, 2)


def slot_of(relative):
    odd_even = jnp.where(relative < 4, 2 * relative, 2 * (8 - relative) - 1)
    return jnp.where(relative == 4, 7, jnp.where(relative == 0, 0, odd_even))


def store_heads(out, acc, n):
    kind, head = n // 2, n % 2
    for doc in range(2):
        out[doc * 2 + head, :ROWS, kind * HEAD_DIM : (kind + 1) * HEAD_DIM] = acc[doc * ROWS : (doc + 1) * ROWS]


def project_most_kernel(where, *refs):
    enc, own, other = refs[:7], refs[7:12], refs[12:17]
    out, w_left, enc_all, w_all, sem_e, sem_w = refs[17:]
    y, x, core = where[0], where[1], where[2]
    parts = []
    for side, blocks in enumerate((own, other)):
        of_core = core if side == 0 else 1 - core
        for piece, ref in enumerate(blocks):
            block = lax.rem(x + X_OFFSETS[piece], 4)
            for part in range(ref.shape[0] // FEATS):
                within = 1 if piece == 4 else part
                segment = (block * 2 + of_core) * 2 + within
                relative = lax.rem(lax.rem(segment, 8) - y + 8, 8)
                row = (slot_of(relative) * 2 + segment // 8) * FEATS
                parts.append((ref, part * FEATS, pl.multiple_of(row, FEATS)))
    enc_copies = [
        pltpu.make_async_copy(
            ref.at[high],
            enc_all.at[:, :, pl.ds((2 * piece + high) * FEATS, FEATS)],
            sem_e.at[2 * piece + high],
        )
        for piece, ref in enumerate(enc)
        for high in range(2)
    ]
    half = 2 * HEAD_DIM
    w_copies = [
        [
            pltpu.make_async_copy(
                ref.at[pl.ds(start, FEATS), pl.ds(kind * half, half)],
                w_all.at[pl.ds(row, FEATS), pl.ds(kind * half, half)],
                sem_w.at[kind, n],
            )
            for n, (ref, start, row) in enumerate(parts)
        ]
        for kind in range(2)
    ]
    for copy in enc_copies + w_copies[0] + w_copies[1]:
        copy.start()
    for copy in enc_copies:
        copy.wait()
    depth = 2 * len(enc) * FEATS
    lhs = enc_all[...].reshape(2 * ROWS, depth)
    for kind in range(2):
        for copy in w_copies[kind]:
            copy.wait()
        for head in range(2):
            n = 2 * kind + head
            cols = slice(n * HEAD_DIM, (n + 1) * HEAD_DIM)
            out[:, cols] = jnp.dot(lhs, w_all[:depth, cols], preferred_element_type=jnp.float32)
    for high in range(2):
        w_left[high] = w_all[depth + high * FEATS : depth + (high + 1) * FEATS, :]


def project_most(where, enc, own, other):
    return pl.pallas_call(
        project_most_kernel,
        out_shape=(
            jax.ShapeDtypeStruct((2 * ROWS, 4 * HEAD_DIM), jnp.float32),
            jax.ShapeDtypeStruct((2, FEATS, 4 * HEAD_DIM), jnp.bfloat16),
        ),
        in_specs=[SMEM] + [ANY] * 17,
        out_specs=(VMEM, VMEM),
        scratch_shapes=[
            pltpu.VMEM((2, ROWS, 14 * FEATS), jnp.bfloat16),
            pltpu.VMEM((4096, 4 * HEAD_DIM), jnp.bfloat16),
            pltpu.SemaphoreType.DMA((14,)),
            pltpu.SemaphoreType.DMA((2, 16)),
        ],
        compiler_params=pltpu.CompilerParams(vmem_limit_bytes=32 * 2**20),
        cost_estimate=pl.CostEstimate(
            flops=2 * 512 * 3584 * 1024, bytes_accessed=14 * 2**20, transcendentals=0
        ),
        name="project_most",
    )(where, *enc, *own, *other)


def project_rest_kernel(first, second, partial, w_left, queries, out):
    first_rows = first[...].reshape(2 * ROWS, FEATS)
    second_rows = second[...].reshape(2 * ROWS, FEATS)
    for n in range(4):
        cols = slice(n * HEAD_DIM, (n + 1) * HEAD_DIM)
        acc = jnp.dot(first_rows, w_left[0, :, cols], preferred_element_type=jnp.float32)
        acc += jnp.dot(second_rows, w_left[1, :, cols], preferred_element_type=jnp.float32)
        store_heads(out, (acc + partial[:, cols]).astype(jnp.bfloat16), n)
    for doc in range(2):
        for head in range(2):
            cols = slice(head * HEAD_DIM, (head + 1) * HEAD_DIM)
            for part in range(2):
                out[doc * 2 + head, ROWS:, part * HEAD_DIM : (part + 1) * HEAD_DIM] = queries[
                    0, doc, part * 64 : (part + 1) * 64, cols
                ]


def project_rest(first, second, partial, w_left, queries):
    return pl.pallas_call(
        project_rest_kernel,
        out_shape=jax.ShapeDtypeStruct((4, ROWS + 64, 2 * HEAD_DIM), jnp.bfloat16),
        in_specs=[VMEM] * 5,
        out_specs=VMEM,
        compiler_params=pltpu.CompilerParams(vmem_limit_bytes=32 * 2**20),
        cost_estimate=pl.CostEstimate(
            flops=2 * 512 * 512 * 1024, bytes_accessed=5 * 2**20, transcendentals=0
        ),
        name="project_rest",
    )(first, second, partial, w_left, queries)


def attend_half(where, lengths, ref, of, q):
    length = lengths[where[1] // 2]
    scores = []
    for p in range(4):
        s = lax.dot_general(
            q, ref[p, :ROWS, :HEAD_DIM], (((1,), (1,)), ((), ())), preferred_element_type=jnp.float32
        )
        place = (p * 2 + of) * ROWS + lax.broadcasted_iota(jnp.int32, (1, ROWS), 1)
        scores.append(jnp.where(place < length, s * (1.0 / math.sqrt(HEAD_DIM)), -jnp.inf))
    top = jnp.maximum(jnp.maximum(scores[0], scores[1]), jnp.maximum(scores[2], scores[3]))
    top = jnp.max(top, axis=1, keepdims=True)
    total, summed = None, None
    for p, s in enumerate(scores):
        w = jnp.exp(s - top)
        total = w if total is None else total + w
        o = jnp.dot(w.astype(jnp.bfloat16), ref[p, :ROWS, HEAD_DIM:], preferred_element_type=jnp.float32)
        summed = o if summed is None else summed + o
    return top, jnp.sum(total, axis=1, keepdims=True), summed


def query_of(mine, chunk):
    return jnp.concatenate([mine[chunk, ROWS:, :HEAD_DIM], mine[chunk, ROWS:, HEAD_DIM:]], axis=0)


def attend_mine_kernel(where, lengths, mine, top, total, summed):
    for chunk in range(4):
        t, n, o = attend_half(where, lengths, mine, where[2], query_of(mine, chunk))
        top[chunk] = jnp.broadcast_to(t, (128, 128))
        total[chunk] = jnp.broadcast_to(n, (128, 128))
        summed[chunk] = o


def attend_theirs_kernel(where, lengths, mine, theirs, top, total, summed, out):
    for chunk in range(4):
        t, n, o = attend_half(where, lengths, theirs, 1 - where[2], query_of(mine, chunk))
        before = top[chunk][:, :1]
        both = jnp.maximum(before, t)
        old, new = jnp.exp(before - both), jnp.exp(t - both)
        out[chunk] = ((old * summed[chunk] + new * o) / (old * total[chunk][:, :1] + new * n)).astype(jnp.bfloat16)


def attend(where, lengths, mine, theirs):
    cost = pl.CostEstimate(flops=2 * 512 * 2048 * 256, bytes_accessed=2 * 2**20, transcendentals=512 * 1024)
    params = pltpu.CompilerParams(vmem_limit_bytes=32 * 2**20)
    stat = jax.ShapeDtypeStruct((4, 128, 128), jnp.float32)
    state = pl.pallas_call(
        attend_mine_kernel,
        out_shape=(stat, stat, jax.ShapeDtypeStruct((4, 128, HEAD_DIM), jnp.float32)),
        in_specs=[SMEM, SMEM, VMEM],
        out_specs=(VMEM, VMEM, VMEM),
        compiler_params=params,
        cost_estimate=cost,
        name="attend_mine",
    )(where, lengths, mine)
    return pl.pallas_call(
        attend_theirs_kernel,
        out_shape=jax.ShapeDtypeStruct((4, 128, HEAD_DIM), jnp.bfloat16),
        in_specs=[SMEM, SMEM] + [VMEM] * 5,
        out_specs=VMEM,
        compiler_params=params,
        cost_estimate=cost,
        name="attend_theirs",
    )(where, lengths, mine, theirs, *state)


def side_by_side_kernel(parts, out):
    for doc in range(2):
        for head in range(2):
            out[0, doc, :, head * HEAD_DIM : (head + 1) * HEAD_DIM] = parts[doc * 2 + head]


def side_by_side(parts):
    return pl.pallas_call(
        side_by_side_kernel,
        out_shape=jax.ShapeDtypeStruct((1, 2, 128, 2 * HEAD_DIM), jnp.bfloat16),
        in_specs=[VMEM],
        out_specs=VMEM,
        name="side_by_side",
    )(parts)


def on_device(queries, enc_states, key_weight, value_weight, enc_lengths):
    where = jnp.stack([lax.axis_index("y"), lax.axis_index("x"), lax.axis_index("c")])
    weight = jnp.concatenate([key_weight[0], value_weight[0]], axis=1)
    own = ring_of_four(weight)
    other = [shift(block, "c", 1) for block in own]
    enc, (first, second) = ring_of_eight(lax.all_gather(enc_states, "zh"))

    enc[1], enc[2] = in_hbm(enc[1]), in_hbm(enc[2])
    own = own[:3] + [in_hbm(own[3]), in_hbm(own[4])]
    partial, w_left = project_most(where, enc, own, other)
    both = project_rest(first, second, partial, w_left, queries)
    mine = lax.all_to_all(both, "x", 0, 0)
    theirs = shift(mine, "c", 1)
    mixed = attend(where, enc_lengths, mine, theirs)
    return side_by_side(lax.all_to_all(mixed, "x", 0, 0))


def solution(mesh):
    torus = Mesh(mesh.devices.reshape(2, 8, 4, 2, 4), ("zh", "y", "x", "c", "mp"))
    return jax.shard_map(
        on_device,
        mesh=torus,
        in_specs=(
            P(SEGMENT, None, CTX, "mp"),
            P(None, CTX, SEGMENT),
            P(SEGMENT, CTX, "mp"),
            P(SEGMENT, CTX, "mp"),
            P(),
        ),
        out_specs=P(SEGMENT, None, CTX, "mp"),
        check_vma=False,
    )
```
